32 devices in a mesh: groups: 2 (over x), tm: 16 (over z, y, core).
Axes of the slice: x: 2, y: 2, z: 4, core: 2. Of those that a mesh axis runs over, the one named last changes fastest.
Arguments:
- gauge_series: bfloat16 [2048, 8192], P('groups', 'tm'), parts along dimension 0, may hold values from -6 to 6
- gauge_order: int32 [8192], replicated, may hold values from 0 to 8191, each once
- gauge_block: int32 [8192], replicated, may hold values from 0 to 3
- gauge_weight: bfloat16 [8192, 64], replicated, may hold values from -0.125 to 0.125
- filt_trans: float32 [512, 256], P('groups'), parts along dimension 0, may hold values from -2 to 2
- obs_gain: float32 [512, 256], P('groups'), parts along dimension 0, may hold values from -2 to 2
- smooth_gain: float32 [512, 256], P('groups'), parts along dimension 0, may hold values from -2 to 2
Outputs:
- filtered_mean: float32 [2048, 256], P(('groups', 'tm')), parts along dimension 0
- smoothed_mean: float32 [2048, 256], P(('groups', 'tm')), parts along dimension 0
The draws below stay inside these ranges and needn't reach their ends.
There are 2 independent parts, one for each index of `groups`. The reference program is written for one: setup_inputs(seed, part) draws one part's arguments, and reference() takes and returns one part's arrays. A program takes and returns all parts, laid end to end along the dimension named above; an argument that names none is the same for every part. Nothing has to cross between parts.
Inputs may be any that keep to these rules, and one draw needn't show every extreme that they name: `gauge_order`: each gauge appears in exactly one column.
All inputs are finite; a program needn't handle non-finite values.
Results may differ from the reference program's by a relative error of at most 0.0003.
Values may be sent and summed in bfloat16 or wider, within the bound.
A program may use at most 128 MiB of HBM per device.

```python
import math
import jax
import jax.numpy as jnp
from jax import lax

STATES = 256
BLOCK = 64
GAUGES = 8192
NBLK = 4
TIME = 1024


def spectral_pair(key, salt):
    normal_block = jax.random.normal(jax.random.fold_in(key, salt), (STATES, STATES), jnp.float32)
    eigen_basis, unused_factor = jnp.linalg.qr(normal_block)
    low_rate = math.log(0.2 / TIME)
    high_rate = math.log(1.0 / 30.0)
    log_rates = jax.random.uniform(jax.random.fold_in(key, salt + 1), (STATES,), jnp.float32, low_rate, high_rate)
    skew_block = jax.random.normal(jax.random.fold_in(key, salt + 2), (STATES, STATES), jnp.float32) * (0.4 / math.sqrt(STATES))
    mixing = jnp.eye(STATES, dtype=jnp.float32) + jnp.triu(skew_block, 1)
    return (eigen_basis, mixing, jnp.exp(log_rates))


def conjugated(eigen_basis, mixing, factor):
    scaled = mixing * factor[None, :]
    similar = lax.linalg.triangular_solve(mixing, scaled, left_side=False, lower=False)
    return jnp.dot(jnp.dot(eigen_basis, similar), eigen_basis.T).astype(jnp.float32)


def draw_filt_trans(key, part):
    eigen_basis, mixing, decay_rates = spectral_pair(key, 11)
    return conjugated(eigen_basis, mixing, jnp.exp(-decay_rates))


def draw_obs_gain(key, part):
    eigen_basis, mixing, decay_rates = spectral_pair(key, 11)
    return conjugated(eigen_basis, mixing, jnp.sqrt(-jnp.expm1(-2.0 * decay_rates)))


def draw_smooth_gain(key, part):
    eigen_basis, mixing, decay_rates = spectral_pair(key, 21)
    return conjugated(eigen_basis, mixing, jnp.exp(-decay_rates))


def place_ends(entries, stream_key, smallest, high):
    spot = [jax.random.randint(jax.random.fold_in(stream_key, axis), (), 0, length) for axis, length in enumerate(entries.shape)]
    main_axis = entries.shape.index(max(entries.shape))
    beside = spot[:main_axis] + [(spot[main_axis] + 1) % entries.shape[main_axis]] + spot[main_axis + 1:]
    return entries.at[tuple(spot)].set(smallest).at[tuple(beside)].set(high)


def shard_levels(rng, shape, pieces, low, largest):
    level, own = 1.0, jax.random.fold_in(rng, 6)
    for position, shards_of in pieces:
        heights = jnp.exp(jax.random.uniform(jax.random.fold_in(own, position), (shards_of,), jnp.float32, low / len(pieces), largest / len(pieces)))
        level = level * jnp.repeat(heights, shape[position] // shards_of).reshape([-1 if axis == position else 1 for axis in range(len(shape))])
    return level


def centred(own_key, shape, scale, limit, cuts=(), held_as=jnp.bfloat16):
    entries = jax.random.normal(own_key, shape, jnp.float32) * scale
    if len(cuts) > 0:
        entries = shard_levels(own_key, shape, cuts, -0.22, 0.18) * entries
    return jnp.clip(entries, min=-limit, max=limit).astype(held_as)


def setup_inputs(seed: int = 0, part: int = 0) -> dict:
    seeds = jax.random.split(jax.random.key(seed), 8)
    part_keys = jax.random.split(jax.random.fold_in(seeds[7], part), 8)
    return {
        "gauge_series": centred(part_keys[0], (TIME, GAUGES), 1.0, 6.0, ((1, 16),)),
        "gauge_order": jax.random.permutation(seeds[1], GAUGES).astype(jnp.int32),
        "gauge_block": place_ends(jax.random.randint(seeds[2], (GAUGES,), 0, NBLK), jax.random.fold_in(seeds[2], 1), 0, NBLK - 1).astype(jnp.int32),
        "gauge_weight": centred(seeds[3], (GAUGES, BLOCK), (GAUGES // NBLK) ** -0.5, 0.125),
        "filt_trans": draw_filt_trans(jax.random.fold_in(jax.random.fold_in(seeds[7], part), 71), part),
        "obs_gain": draw_obs_gain(jax.random.fold_in(jax.random.fold_in(seeds[7], part), 71), part),
        "smooth_gain": draw_smooth_gain(jax.random.fold_in(jax.random.fold_in(seeds[7], part), 71), part),
    }


PRECISE = lax.Precision.HIGHEST

def apply_rows(values, matrix):
    return lax.dot_general(values.astype(jnp.float32), matrix.astype(jnp.float32), (((1,), (1,)), ((), ())), precision=PRECISE, preferred_element_type=jnp.float32)

def reference(gauge_series, gauge_order, gauge_block, gauge_weight, filt_trans, obs_gain, smooth_gain):
    blocks = jnp.take(gauge_block, gauge_order)
    weights = jnp.take(gauge_weight, gauge_order, axis=0)
    onehot = (blocks[:, None] == jnp.arange(NBLK, dtype=jnp.int32)[None, :]).astype(jnp.bfloat16)
    design = (onehot[:, :, None] * weights[:, None, :]).reshape(GAUGES, STATES)
    information = jnp.dot(gauge_series.astype(jnp.float32), design.astype(jnp.float32), preferred_element_type=jnp.float32)
    inputs = apply_rows(information, obs_gain)

    def forward(previous, current):
        updated = jnp.dot(filt_trans, previous, precision=PRECISE) + current
        return (updated, updated)
    unused_state, filtered = lax.scan(forward, jnp.zeros((STATES,), jnp.float32), inputs)
    blended = filtered - apply_rows(filtered, smooth_gain)
    blended = blended.at[TIME - 1].set(filtered[TIME - 1])

    def backward(previous, current):
        updated = jnp.dot(smooth_gain, previous, precision=PRECISE) + current
        return (updated, updated)
    unused_back, smoothed = lax.scan(backward, jnp.zeros((STATES,), jnp.float32), blended, reverse=True)
    return (filtered, smoothed)
```

```python
import functools

import jax
import jax.numpy as jnp
from jax import lax
from jax.experimental import pallas as pl
from jax.experimental.pallas import tpu as pltpu
from jax.sharding import PartitionSpec as P

MESH = pl.DeviceIdType.MESH
LANES = 128
WIDE = 256
LEVELS = 32704.0


def dot(left, right):
    return jnp.dot(left, right, preferred_element_type=jnp.float32)


def split(values):
    high = values.astype(jnp.bfloat16)
    return high, (values - high.astype(jnp.float32)).astype(jnp.bfloat16)


def matmul3(left, right):
    high, low = split(left)
    top, rest = split(right)
    rows = left.shape[0]
    both = dot(jnp.concatenate([high, low], 0), top)
    return dot(high, rest) + both[:rows] + both[rows:]


def applied(values, rest):
    return values - matmul3(values, rest)


def eye(size):
    row = lax.broadcasted_iota(jnp.int32, (size, size), 0)
    column = lax.broadcasted_iota(jnp.int32, (size, size), 1)
    return jnp.where(row == column, 1.0, 0.0)


def shift(values, offset):
    rows = values.shape[0]
    moved = pltpu.roll(values, offset % rows, 0)
    place = lax.broadcasted_iota(jnp.int32, values.shape, 0)
    kept = place >= offset if offset > 0 else place < rows + offset
    return jnp.where(kept, moved, 0.0)


def put_row(values, row, where):
    place = lax.broadcasted_iota(jnp.int32, values.shape, 0)
    return values + jnp.where(place == where, row, 0.0)


def bit_reversed(number, bits):
    return int(format(number, "b").zfill(bits)[::-1], 2) if bits else 0


def kernel(
    devices,
    series_any,
    order_any,
    block_any,
    weight_any,
    filt_any,
    gain_any,
    back_any,
    filtered_a,
    filtered_b,
    smoothed_a,
    smoothed_b,
    series,
    order,
    block,
    weight,
    filt_in,
    gain_in,
    back_in,
    info,
    half,
    quant,
    scale,
    land,
    scale_land,
    pair,
    ends,
    starts,
    carry,
    carry_land,
    filt,
    back,
    crossed,
    enter,
    gain,
    load,
    sib_send,
    sib_recv,
    info_send,
    info_recv,
    scale_send,
    scale_recv,
    carry_send,
    carry_recv,
):
    me = lax.axis_index("tm")
    core = lax.rem(me, 2)
    chip = lax.div(me, 2)
    sibling = me + 1 - 2 * core
    chips = devices // 2
    steps, columns = series.shape
    length = steps // devices
    states = filt_in.shape[0]
    span, gauges = weight.shape
    depth = length.bit_length() - 1
    scans = devices.bit_length() - 1
    halves = states // LANES

    loads = []
    for n, (source, target) in enumerate(
        (
            (order_any.at[me], order),
            (block_any, block),
            (weight_any, weight),
            (filt_any, filt_in),
            (back_any, back_in),
            (series_any, series),
            (gain_any, gain_in),
        )
    ):
        copy = pltpu.make_async_copy(source, target, load.at[n])
        copy.start()
        loads.append(copy)
    barrier = pltpu.get_barrier_semaphore()
    for k in range(1, devices):
        pl.semaphore_signal(
            barrier, inc=1, device_id={"tm": lax.rem(me + k, devices)}, device_id_type=MESH
        )

    def power(h):
        filt[h + 1] = 2.0 * filt[h] - matmul3(filt[h], filt[h])
        back[h + 1] = 2.0 * back[h] - matmul3(back[h], back[h])

    def cross(h):
        crossed[h] = applied(enter[...], back[h])
        enter[...] = enter[...] + crossed[h] - matmul3(filt[h], crossed[h])

    loads[0].wait()
    loads[1].wait()
    number = order[...]
    upper = lax.div(number, WIDE)
    lower = lax.rem(number, WIDE)
    spot = lax.broadcasted_iota(jnp.int32, (WIDE, columns), 0)
    onehot = jnp.where(spot == lower, 1.0, 0.0).astype(jnp.bfloat16)
    parts = gauges // WIDE
    table = jnp.concatenate(
        [block[pl.ds(j, parts, stride=WIDE // LANES)] for j in range(WIDE // LANES)], 1
    )
    found = dot(table.astype(jnp.float32).astype(jnp.bfloat16), onehot)
    spot = lax.broadcasted_iota(jnp.int32, (parts, columns), 0)
    kind = jnp.sum(jnp.where(spot == upper, found, 0.0), 0, keepdims=True)
    for copy in loads[2:5]:
        copy.wait()
    weights = jnp.zeros((span, columns), jnp.float32)
    together = 8
    for base in range(0, parts, together):
        rows = [
            weight[:, (base + i) * WIDE : (base + i + 1) * WIDE]
            for i in range(min(together, parts - base))
        ]
        found = dot(jnp.concatenate(rows, 0), onehot)
        for i in range(len(rows)):
            weights = weights + jnp.where(
                upper == base + i, found[i * span : (i + 1) * span], 0.0
            )
    design = jnp.concatenate(
        [jnp.where(kind == float(k), weights, 0.0) for k in range(states // span)], 0
    ).astype(jnp.bfloat16)
    filt[0] = eye(states) - filt_in[...].T
    back[0] = eye(states) - back_in[...].T
    enter[...] = back[0] - matmul3(filt[0], back[0])
    power(0)

    for copy in loads[5:]:
        copy.wait()
    gain[:, :states] = gain_in[...].T
    gain[:, states:] = matmul3(gain[:, :states], back[0])
    sib = []
    chunk = min(steps, 4 * length)
    for base in range(0, steps, chunk):
        partial = lax.dot_general(
            series[base : base + chunk],
            design,
            (((1,), (1,)), ((), ())),
            preferred_element_type=jnp.float32,
        )
        for b in range(base // length, (base + chunk) // length):
            row = b * length - base
            at = ((b % 2) * chips + b // 2) * length
            for j in range(halves):
                info[j, at : at + length] = partial[
                    row : row + length, j * LANES : (j + 1) * LANES
                ]
        if base == 0:
            pl.semaphore_wait(barrier, devices - 1)
        for t in range(base // (2 * length), (base + chunk) // (2 * length)):
            rows = pl.ds(pl.multiple_of(((1 - core) * chips + t) * length, length), length)
            copy = pltpu.make_async_remote_copy(
                src_ref=info.at[:, rows],
                dst_ref=half.at[t],
                send_sem=sib_send.at[t],
                recv_sem=sib_recv.at[t],
                device_id={"tm": sibling},
                device_id_type=MESH,
            )
            copy.start()
            sib.append(copy)
    cross(0)
    for h in range(1, 3):
        power(h)
        cross(h)

    def summed(t):
        rows = pl.ds(pl.multiple_of(((1 - core) * chips + t) * length, length), length)
        pltpu.make_async_remote_copy(
            src_ref=info.at[:, rows],
            dst_ref=half.at[t],
            send_sem=sib_send.at[t],
            recv_sem=sib_recv.at[t],
            device_id={"tm": sibling},
            device_id_type=MESH,
        ).wait_recv()
        rows = pl.ds(pl.multiple_of((core * chips + t) * length, length), length)
        both = info[:, rows] + half[t]
        pair[:, pl.ds(pl.multiple_of(t * length, length), length)] = both
        return jnp.concatenate([both[j] for j in range(halves)], 1)

    sends = []
    for k in range(chips - 1):
        t = k + lax.div(k - chip + chips, chips)
        values = summed(t)
        largest = jnp.maximum(jnp.max(jnp.abs(values), 0, keepdims=True), 1e-30)
        quant[k] = jnp.round(values * (LEVELS / largest)).astype(jnp.int32).astype(jnp.int16)
        scale[k] = largest * (1.0 / LEVELS)
        for source, target, send, recv in (
            (quant, land, info_send, info_recv),
            (scale, scale_land, scale_send, scale_recv),
        ):
            copy = pltpu.make_async_remote_copy(
                src_ref=source.at[k],
                dst_ref=target.at[chip],
                send_sem=send.at[k],
                recv_sem=recv.at[chip],
                device_id={"tm": 2 * t + core},
                device_id_type=MESH,
            )
            copy.start()
            sends.append(copy)
    total = summed(chip)

    for h in range(3, depth):
        power(h)
        cross(h)
    for t in range(length):
        at = bit_reversed(t, depth) * chips
        for j in range(halves):
            ends[at : at + chips, j * LANES : (j + 1) * LANES] = pair[
                j, pl.ds(t, chips, stride=length)
            ]
    rows = chips * length
    part = min(rows, 512)
    for base in range(0, rows, part):
        ready = matmul3(ends[base : base + part], gain[...])
        ends[base : base + part] = ready[:, :states]
        starts[base : base + part] = ready[:, states:]
    for h in range(depth, depth + scans - 1):
        power(h)
    for h in range(depth):
        rows //= 2
        part = min(rows, 512)
        for base in range(0, rows, part):
            here = slice(base, base + part)
            there = slice(rows + base, rows + base + part)
            left = ends[here]
            starts[here] = (
                starts[here] + applied(starts[there], back[h]) + matmul3(left, crossed[h])
            )
            ends[here] = ends[there] + applied(left, filt[h])

    def spread(values):
        return jnp.concatenate(
            [
                jnp.where(core == b % 2, values[b // 2 : b // 2 + 1], 0.0)
                for b in range(devices)
            ],
            0,
        )

    reached = spread(ends[:chips])
    opened = spread(starts[:chips])
    for h in range(scans):
        reached = reached + applied(shift(reached, 1 << h), filt[depth + h])
    arrive = shift(reached, 1)
    final = reached[devices - 1 : devices]
    leaving = put_row(jnp.zeros_like(opened), final, devices - 1)
    opened = opened + matmul3(arrive, enter[...]) + applied(leaving, back[depth])
    for h in range(scans):
        opened = opened + applied(shift(opened, -(1 << h)), back[depth + h])
    arrive_back = put_row(shift(opened, -1), final, devices - 1)
    for b in range(devices):
        carry[b, 0:1] = arrive[b : b + 1]
        carry[b, 1:2] = arrive_back[b : b + 1]

    carries = []
    for k in range(devices - 1):
        target = k + lax.div(k - me + devices, devices)
        copy = pltpu.make_async_remote_copy(
            src_ref=carry.at[target],
            dst_ref=carry_land.at[me],
            send_sem=carry_send.at[k],
            recv_sem=carry_recv.at[me],
            device_id={"tm": target},
            device_id_type=MESH,
        )
        copy.start()
        carries.append(copy)

    for k in range(chips - 1):
        s = k + lax.div(k - chip + chips, chips)
        for source, target, send, recv in (
            (quant, land, info_send, info_recv),
            (scale, scale_land, scale_send, scale_recv),
        ):
            pltpu.make_async_remote_copy(
                src_ref=source.at[k],
                dst_ref=target.at[s],
                send_sem=send.at[k],
                recv_sem=recv.at[s],
                device_id={"tm": 2 * s + core},
                device_id_type=MESH,
            ).wait_recv()
        total = total + land[s].astype(jnp.int32).astype(jnp.float32) * scale_land[s]
    inputs = matmul3(total, gain[:, :states])

    entering = carry[me]
    for k in range(devices - 1):
        source = k + lax.div(k - me + devices, devices)
        pltpu.make_async_remote_copy(
            src_ref=carry.at[source],
            dst_ref=carry_land.at[source],
            send_sem=carry_send.at[k],
            recv_sem=carry_recv.at[source],
            device_id={"tm": source},
            device_id_type=MESH,
        ).wait_recv()
        entering = entering + carry_land[source]

    first = put_row(jnp.zeros_like(inputs), entering[0:1], 0)
    filtered = inputs + applied(first, filt[0])
    for h in range(depth - 1):
        filtered = filtered + applied(shift(filtered, 1 << h), filt[h])
    more = applied(shift(filtered, 1 << (depth - 1)), filt[depth - 1])
    filtered_a[...] = filtered
    filtered_b[...] = more
    filtered = filtered + more
    following = put_row(jnp.zeros_like(inputs), entering[1:2], length - 1)
    smoothed = following + matmul3(filtered - following, back[0])
    for h in range(depth - 1):
        smoothed = smoothed + applied(shift(smoothed, -(1 << h)), back[h])
    smoothed_a[...] = smoothed
    smoothed_b[...] = applied(shift(smoothed, -(1 << (depth - 1))), back[depth - 1])

    for copy in sib + sends + carries:
        copy.wait_send()


def per_device(
    gauge_series, gauge_order, gauge_block, gauge_weight, filt_trans, obs_gain, smooth_gain
):
    devices = lax.axis_size("tm")
    steps, columns = gauge_series.shape
    gauges, span = gauge_weight.shape
    states = filt_trans.shape[0]
    length = steps // devices
    chips = devices // 2
    depth = length.bit_length() - 1
    scans = devices.bit_length() - 1
    halves = states // LANES
    out = pltpu.VMEM((length, states), jnp.float32)
    square = (states, states)
    filtered_a, filtered_b, smoothed_a, smoothed_b = pl.pallas_call(
        functools.partial(kernel, devices),
        out_shape=(out,) * 4,
        in_specs=[pl.BlockSpec(memory_space=pl.ANY)] * 7,
        out_specs=[pl.BlockSpec(memory_space=pltpu.VMEM)] * 4,
        scratch_shapes=[
            pltpu.VMEM((steps, columns), jnp.bfloat16),
            pltpu.VMEM((1, columns), jnp.int32),
            pltpu.VMEM((gauges // LANES, LANES), jnp.int32),
            pltpu.VMEM((span, gauges), jnp.bfloat16),
            pltpu.VMEM(square, jnp.float32),
            pltpu.VMEM(square, jnp.float32),
            pltpu.VMEM(square, jnp.float32),
            pltpu.VMEM((halves, steps, LANES), jnp.float32),
            pltpu.VMEM((chips, halves, length, LANES), jnp.float32),
            pltpu.VMEM((chips, length, states), jnp.int16),
            pltpu.VMEM((chips, 1, states), jnp.float32),
            pltpu.VMEM((chips, length, states), jnp.int16),
            pltpu.VMEM((chips, 1, states), jnp.float32),
            pltpu.VMEM((halves, chips * length, LANES), jnp.float32),
            pltpu.VMEM((chips * length, states), jnp.float32),
            pltpu.VMEM((chips * length, states), jnp.float32),
            pltpu.VMEM((devices, 2, states), jnp.float32),
            pltpu.VMEM((devices, 2, states), jnp.float32),
            pltpu.VMEM((depth + scans,) + square, jnp.float32),
            pltpu.VMEM((depth + scans,) + square, jnp.float32),
            pltpu.VMEM((depth,) + square, jnp.float32),
            pltpu.VMEM(square, jnp.float32),
            pltpu.VMEM((states, 2 * states), jnp.float32),
            pltpu.SemaphoreType.DMA((7,)),
            pltpu.SemaphoreType.DMA((chips,)),
            pltpu.SemaphoreType.DMA((chips,)),
            pltpu.SemaphoreType.DMA((chips,)),
            pltpu.SemaphoreType.DMA((chips,)),
            pltpu.SemaphoreType.DMA((chips,)),
            pltpu.SemaphoreType.DMA((chips,)),
            pltpu.SemaphoreType.DMA((devices,)),
            pltpu.SemaphoreType.DMA((devices,)),
        ],
        compiler_params=pltpu.CompilerParams(
            collective_id=0, has_side_effects=True, vmem_limit_bytes=58 << 20
        ),
    )(
        gauge_series,
        gauge_order.reshape(devices, 1, columns),
        gauge_block.reshape(-1, LANES),
        gauge_weight.T,
        filt_trans,
        obs_gain,
        smooth_gain,
    )
    return filtered_a + filtered_b, smoothed_a + smoothed_b


def solution(mesh):
    placed = (
        P("groups", "tm"),
        P(),
        P(),
        P(),
        P("groups", None),
        P("groups", None),
        P("groups", None),
    )
    return jax.shard_map(
        per_device,
        mesh=mesh,
        in_specs=placed,
        out_specs=(P(("groups", "tm"), None), P(("groups", "tm"), None)),
        check_vma=False,
    )
```

```python
import functools

import jax
import jax.numpy as jnp
from jax import lax
from jax.experimental import pallas as pl
from jax.experimental.pallas import tpu as pltpu
from jax.sharding import PartitionSpec as P

MESH = pl.DeviceIdType.MESH
LANES = 128
WIDE = 256
LEVELS = 32704.0


def dot(left, right):
    return jnp.dot(left, right, preferred_element_type=jnp.float32)


def split(values):
    high = values.astype(jnp.bfloat16)
    return high, (values - high.astype(jnp.float32)).astype(jnp.bfloat16)


def product(left, right):
    high, low = left
    top, rest = right
    rows = high.shape[0]
    both = dot(jnp.concatenate([high, low], 0), top)
    return dot(high, rest) + both[:rows] + both[rows:]


def matmul3(left, right):
    return product(split(left), right)


def applied(values, right):
    return values - matmul3(values, right)


def eye(size):
    row = lax.broadcasted_iota(jnp.int32, (size, size), 0)
    column = lax.broadcasted_iota(jnp.int32, (size, size), 1)
    return jnp.where(row == column, 1.0, 0.0)


def shift(values, offset):
    rows = values.shape[0]
    moved = pltpu.roll(values, offset % rows, 0)
    place = lax.broadcasted_iota(jnp.int32, values.shape, 0)
    kept = place >= offset if offset > 0 else place < rows + offset
    return jnp.where(kept, moved, 0.0)


def put_row(values, row, where):
    place = lax.broadcasted_iota(jnp.int32, values.shape, 0)
    return values + jnp.where(place == where, row, 0.0)


def bit_reversed(number, bits):
    return int(format(number, "b").zfill(bits)[::-1], 2) if bits else 0


def kernel(
    devices,
    series_any,
    order_any,
    block_any,
    weight_any,
    filt_any,
    gain_any,
    back_any,
    filtered_a,
    filtered_b,
    smoothed_b,
    series,
    order,
    block,
    weight,
    filt_in,
    gain_in,
    back_in,
    info,
    half,
    quant,
    scale,
    land,
    scale_land,
    pair,
    ends,
    starts,
    carry,
    carry_land,
    filt,
    back,
    crossed,
    enter,
    gain,
    now,
    load,
    sib_send,
    sib_recv,
    info_send,
    info_recv,
    scale_send,
    scale_recv,
    carry_send,
    carry_recv,
):
    me = lax.axis_index("tm")
    core = lax.rem(me, 2)
    chip = lax.div(me, 2)
    sibling = me + 1 - 2 * core
    chips = devices // 2
    steps, columns = series.shape
    length = steps // devices
    states = filt_in.shape[0]
    span, gauges = weight.shape
    depth = length.bit_length() - 1
    scans = devices.bit_length() - 1
    halves = states // LANES

    loads = []
    for n, (source, target) in enumerate(
        (
            (filt_any, filt_in),
            (back_any, back_in),
            (order_any.at[me], order),
            (block_any, block),
            (weight_any, weight),
            (series_any, series),
            (gain_any, gain_in),
        )
    ):
        copy = pltpu.make_async_copy(source, target, load.at[n])
        copy.start()
        loads.append(copy)
    barrier = pltpu.get_barrier_semaphore()
    for k in range(1, devices):
        pl.semaphore_signal(
            barrier, inc=1, device_id={"tm": lax.rem(me + k, devices)}, device_id_type=MESH
        )

    def keep(ref, h, values):
        ref[h, 0], ref[h, 1] = split(values)

    def of(ref, h):
        return ref[h, 0], ref[h, 1]

    def power(h):
        for n, ref in enumerate((filt, back)):
            now[n] = 2.0 * now[n] - product(of(ref, h), of(ref, h))
            keep(ref, h + 1, now[n])

    def cross(h):
        now[3] = now[2] - product(of(enter, h), of(back, h))
        keep(crossed, h, now[3])

    def joined(h):
        now[2] = now[2] + now[3] - product(of(filt, h), of(crossed, h))
        keep(enter, h + 1, now[2])

    todo = []
    for k in range(max(2 * depth, depth + scans - 1)):
        if k < depth + scans - 1:
            todo.append((power, k))
        if k < 2 * depth:
            todo.append((joined if k % 2 else cross, k // 2))

    def advance(count=2):
        for work, h in todo[:count]:
            work(h)
        del todo[:count]

    loads[0].wait()
    loads[1].wait()
    now[0] = eye(states) - filt_in[...].T
    now[1] = eye(states) - back_in[...].T
    keep(filt, 0, now[0])
    keep(back, 0, now[1])
    now[2] = now[1] - product(of(filt, 0), of(back, 0))
    keep(enter, 0, now[2])
    advance()

    for copy in loads[2:]:
        copy.wait()
    number = order[...]
    upper = lax.div(number, WIDE)
    lower = lax.rem(number, WIDE)
    spot = lax.broadcasted_iota(jnp.int32, (WIDE, columns), 0)
    onehot = jnp.where(spot == lower, 1.0, 0.0).astype(jnp.bfloat16)
    parts = gauges // WIDE
    table = jnp.concatenate(
        [block[pl.ds(j, parts, stride=WIDE // LANES)] for j in range(WIDE // LANES)], 1
    )
    found = dot(table.astype(jnp.float32).astype(jnp.bfloat16), onehot)
    spot = lax.broadcasted_iota(jnp.int32, (parts, columns), 0)
    kind = jnp.sum(jnp.where(spot == upper, found, 0.0), 0, keepdims=True)
    weights = jnp.zeros((span, columns), jnp.float32)
    together = 8
    for base in range(0, parts, together):
        rows = [
            weight[:, (base + i) * WIDE : (base + i + 1) * WIDE]
            for i in range(min(together, parts - base))
        ]
        found = dot(jnp.concatenate(rows, 0), onehot)
        for i in range(len(rows)):
            weights = weights + jnp.where(
                upper == base + i, found[i * span : (i + 1) * span], 0.0
            )
        if base % (2 * together):
            advance()
    design = jnp.concatenate(
        [jnp.where(kind == float(k), weights, 0.0) for k in range(states // span)], 0
    ).astype(jnp.bfloat16)
    chunk = min(steps, 4 * length)
    for base in range(0, steps, chunk):
        partial = lax.dot_general(
            series[base : base + chunk],
            design,
            (((1,), (1,)), ((), ())),
            preferred_element_type=jnp.float32,
        )
        for b in range(base // length, (base + chunk) // length):
            row = b * length - base
            at = ((b % 2) * chips + b // 2) * length
            for j in range(halves):
                info[j, at : at + length] = partial[
                    row : row + length, j * LANES : (j + 1) * LANES
                ]
        if base == chunk:
            advance()
    pl.semaphore_wait(barrier, devices - 1)
    sib = []
    for t in range(chips):
        rows = pl.ds(pl.multiple_of(((1 - core) * chips + t) * length, length), length)
        copy = pltpu.make_async_remote_copy(
            src_ref=info.at[:, rows],
            dst_ref=half.at[t],
            send_sem=sib_send.at[t],
            recv_sem=sib_recv.at[t],
            device_id={"tm": sibling},
            device_id_type=MESH,
        )
        copy.start()
        sib.append(copy)
    tune = gain_in[...].T
    keep(gain, 0, tune)
    keep(gain, 1, product(of(gain, 0), of(back, 0)))
    advance(4)

    def summed(t):
        rows = pl.ds(pl.multiple_of(((1 - core) * chips + t) * length, length), length)
        pltpu.make_async_remote_copy(
            src_ref=info.at[:, rows],
            dst_ref=half.at[t],
            send_sem=sib_send.at[t],
            recv_sem=sib_recv.at[t],
            device_id={"tm": sibling},
            device_id_type=MESH,
        ).wait_recv()
        rows = pl.ds(pl.multiple_of((core * chips + t) * length, length), length)
        both = info[:, rows] + half[t]
        pair[:, pl.ds(pl.multiple_of(t * length, length), length)] = both
        return jnp.concatenate([both[j] for j in range(halves)], 1)

    sends = []
    for k in range(chips - 1):
        t = k + lax.div(k - chip + chips, chips)
        values = summed(t)
        largest = jnp.maximum(jnp.max(jnp.abs(values), 0, keepdims=True), 1e-30)
        quant[k] = jnp.round(values * (LEVELS / largest)).astype(jnp.int32).astype(jnp.int16)
        scale[k] = largest * (1.0 / LEVELS)
        for source, target, send, recv in (
            (quant, land, info_send, info_recv),
            (scale, scale_land, scale_send, scale_recv),
        ):
            copy = pltpu.make_async_remote_copy(
                src_ref=source.at[k],
                dst_ref=target.at[chip],
                send_sem=send.at[k],
                recv_sem=recv.at[chip],
                device_id={"tm": 2 * t + core},
                device_id_type=MESH,
            )
            copy.start()
            sends.append(copy)
    total = summed(chip)

    for t in range(length):
        at = bit_reversed(t, depth) * chips
        for j in range(halves):
            ends[at : at + chips, j * LANES : (j + 1) * LANES] = pair[
                j, pl.ds(t, chips, stride=length)
            ]
    advance()
    rows = chips * length
    part = min(rows, 512)
    for base in range(0, rows, part):
        left = split(ends[base : base + part])
        ends[base : base + part] = product(left, of(gain, 0))
        starts[base : base + part] = product(left, of(gain, 1))
    advance()
    for h in range(depth):
        rows //= 2
        part = min(rows, 512)
        for base in range(0, rows, part):
            here = slice(base, base + part)
            there = slice(rows + base, rows + base + part)
            left = split(ends[here])
            starts[here] = (
                starts[here]
                + applied(starts[there], of(back, h))
                + product(left, of(crossed, h))
            )
            ends[here] = ends[there] + ends[here] - product(left, of(filt, h))
        advance()
    advance(len(todo))

    def spread(values):
        return jnp.concatenate(
            [
                jnp.where(core == b % 2, values[b // 2 : b // 2 + 1], 0.0)
                for b in range(devices)
            ],
            0,
        )

    reached = spread(ends[:chips])
    opened = spread(starts[:chips])
    for h in range(scans):
        reached = reached + applied(shift(reached, 1 << h), of(filt, depth + h))
    arrive = shift(reached, 1)
    final = reached[devices - 1 : devices]
    leaving = put_row(jnp.zeros_like(opened), final, devices - 1)
    opened = opened + matmul3(arrive, of(enter, depth)) + applied(leaving, of(back, depth))
    for h in range(scans):
        opened = opened + applied(shift(opened, -(1 << h)), of(back, depth + h))
    arrive_back = put_row(shift(opened, -1), final, devices - 1)
    for b in range(devices):
        carry[b, 0:1] = arrive[b : b + 1]
        carry[b, 1:2] = arrive_back[b : b + 1]

    carries = []
    for k in range(devices - 1):
        target = k + lax.div(k - me + devices, devices)
        copy = pltpu.make_async_remote_copy(
            src_ref=carry.at[target],
            dst_ref=carry_land.at[me],
            send_sem=carry_send.at[k],
            recv_sem=carry_recv.at[me],
            device_id={"tm": target},
            device_id_type=MESH,
        )
        copy.start()
        carries.append(copy)

    for k in range(chips - 1):
        s = k + lax.div(k - chip + chips, chips)
        for source, target, send, recv in (
            (quant, land, info_send, info_recv),
            (scale, scale_land, scale_send, scale_recv),
        ):
            pltpu.make_async_remote_copy(
                src_ref=source.at[k],
                dst_ref=target.at[s],
                send_sem=send.at[k],
                recv_sem=recv.at[s],
                device_id={"tm": 2 * s + core},
                device_id_type=MESH,
            ).wait_recv()
        total = total + land[s].astype(jnp.int32).astype(jnp.float32) * scale_land[s]
    ready = split(total)
    tails = [product(ready, of(gain, 0))]
    heads = [product(ready, of(gain, 1))]
    for h in range(depth - 1):
        inner = shift(tails[h], 1 - (1 << h)) if h else tails[h]
        heads.append(
            heads[h] + applied(shift(heads[h], -(1 << h)), of(back, h)) + matmul3(inner, of(crossed, h))
        )
        tails.append(tails[h] + applied(shift(tails[h], 1 << h), of(filt, h)))

    entering = carry[me]
    for k in range(devices - 1):
        source = k + lax.div(k - me + devices, devices)
        pltpu.make_async_remote_copy(
            src_ref=carry.at[source],
            dst_ref=carry_land.at[source],
            send_sem=carry_send.at[k],
            recv_sem=carry_recv.at[source],
            device_id={"tm": source},
            device_id_type=MESH,
        ).wait_recv()
        entering = entering + carry_land[source]

    place = lax.broadcasted_iota(jnp.int32, (length, states), 0)
    before = jnp.where(place == 0, entering[0:1], 0.0)
    after = jnp.where(place == length - 1, entering[1:2], 0.0)
    for h in reversed(range(depth)):
        offset = lax.rem(place, 2 << h)
        middle = shift(tails[h], 1) + applied(shift(before, 1 << h), of(filt, h))
        before = jnp.where(offset == 1 << h, middle, before)
        middle = heads[h] + matmul3(before, of(enter, h))
        middle = shift(middle, -1) + applied(shift(after, -(1 << h)), of(back, h))
        after = jnp.where(offset == (1 << h) - 1, middle, after)
    carried = applied(before, of(filt, 0))
    filtered_a[...] = tails[0]
    filtered_b[...] = carried
    smoothed_b[...] = heads[0] - tails[0] + matmul3(before, of(enter, 0)) + applied(after, of(back, 0))

    for copy in sib + sends + carries:
        copy.wait_send()


def per_device(
    gauge_series, gauge_order, gauge_block, gauge_weight, filt_trans, obs_gain, smooth_gain
):
    devices = lax.axis_size("tm")
    steps, columns = gauge_series.shape
    gauges, span = gauge_weight.shape
    states = filt_trans.shape[0]
    length = steps // devices
    chips = devices // 2
    depth = length.bit_length() - 1
    scans = devices.bit_length() - 1
    halves = states // LANES
    out = pltpu.VMEM((length, states), jnp.float32)
    square = (states, states)
    filtered_a, filtered_b, smoothed_b = pl.pallas_call(
        functools.partial(kernel, devices),
        out_shape=(out,) * 3,
        in_specs=[pl.BlockSpec(memory_space=pl.ANY)] * 7,
        out_specs=[pl.BlockSpec(memory_space=pltpu.VMEM)] * 3,
        scratch_shapes=[
            pltpu.VMEM((steps, columns), jnp.bfloat16),
            pltpu.VMEM((1, columns), jnp.int32),
            pltpu.VMEM((gauges // LANES, LANES), jnp.int32),
            pltpu.VMEM((span, gauges), jnp.bfloat16),
            pltpu.VMEM(square, jnp.float32),
            pltpu.VMEM(square, jnp.float32),
            pltpu.VMEM(square, jnp.float32),
            pltpu.VMEM((halves, steps, LANES), jnp.float32),
            pltpu.VMEM((chips, halves, length, LANES), jnp.float32),
            pltpu.VMEM((chips, length, states), jnp.int16),
            pltpu.VMEM((chips, 1, states), jnp.float32),
            pltpu.VMEM((chips, length, states), jnp.int16),
            pltpu.VMEM((chips, 1, states), jnp.float32),
            pltpu.VMEM((halves, chips * length, LANES), jnp.float32),
            pltpu.VMEM((chips * length, states), jnp.float32),
            pltpu.VMEM((chips * length, states), jnp.float32),
            pltpu.VMEM((devices, 2, states), jnp.float32),
            pltpu.VMEM((devices, 2, states), jnp.float32),
            pltpu.VMEM((depth + scans, 2) + square, jnp.bfloat16),
            pltpu.VMEM((depth + scans, 2) + square, jnp.bfloat16),
            pltpu.VMEM((depth, 2) + square, jnp.bfloat16),
            pltpu.VMEM((depth + 1, 2) + square, jnp.bfloat16),
            pltpu.VMEM((2, 2) + square, jnp.bfloat16),
            pltpu.VMEM((4,) + square, jnp.float32),
            pltpu.SemaphoreType.DMA((7,)),
            pltpu.SemaphoreType.DMA((chips,)),
            pltpu.SemaphoreType.DMA((chips,)),
            pltpu.SemaphoreType.DMA((chips,)),
            pltpu.SemaphoreType.DMA((chips,)),
            pltpu.SemaphoreType.DMA((chips,)),
            pltpu.SemaphoreType.DMA((chips,)),
            pltpu.SemaphoreType.DMA((devices,)),
            pltpu.SemaphoreType.DMA((devices,)),
        ],
        compiler_params=pltpu.CompilerParams(
            collective_id=0, has_side_effects=True, vmem_limit_bytes=58 << 20
        ),
    )(
        gauge_series,
        gauge_order.reshape(devices, 1, columns),
        gauge_block.reshape(-1, LANES),
        gauge_weight.T,
        filt_trans,
        obs_gain,
        smooth_gain,
    )
    return filtered_a + filtered_b, filtered_a + smoothed_b


def solution(mesh):
    placed = (
        P("groups", "tm"),
        P(),
        P(),
        P(),
        P("groups", None),
        P("groups", None),
        P("groups", None),
    )
    return jax.shard_map(
        per_device,
        mesh=mesh,
        in_specs=placed,
        out_specs=(P(("groups", "tm"), None), P(("groups", "tm"), None)),
        check_vma=False,
    )
```

```python
import functools

import jax
import jax.numpy as jnp
from jax import lax
from jax.experimental import pallas as pl
from jax.experimental.pallas import tpu as pltpu
from jax.sharding import PartitionSpec as P

MESH = pl.DeviceIdType.MESH
LANES = 128
WIDE = 256
LEVELS = 32704.0
GROUP = 8


def dot(left, right):
    return jnp.dot(left, right, preferred_element_type=jnp.float32)


def split(values):
    high = values.astype(jnp.bfloat16)
    return high, (values - high.astype(jnp.float32)).astype(jnp.bfloat16)


def product(left, right):
    high, low = left
    top, rest = right
    rows = high.shape[0]
    both = dot(jnp.concatenate([high, low], 0), top)
    return dot(high, rest) + both[:rows] + both[rows:]


def matmul3(left, right):
    return product(split(left), right)


def applied(values, right):
    return values - matmul3(values, right)


def eye(size):
    row = lax.broadcasted_iota(jnp.int32, (size, size), 0)
    column = lax.broadcasted_iota(jnp.int32, (size, size), 1)
    return jnp.where(row == column, 1.0, 0.0)


def shift(values, offset):
    rows = values.shape[0]
    moved = pltpu.roll(values, offset % rows, 0)
    place = lax.broadcasted_iota(jnp.int32, values.shape, 0)
    kept = place >= offset if offset > 0 else place < rows + offset
    return jnp.where(kept, moved, 0.0)


def put_row(values, row, where):
    place = lax.broadcasted_iota(jnp.int32, values.shape, 0)
    return values + jnp.where(place == where, row, 0.0)


def bit_reversed(number, bits):
    return int(format(number, "b").zfill(bits)[::-1], 2) if bits else 0


def kernel(
    devices,
    series_any,
    order_any,
    block_any,
    weight_any,
    filt_any,
    gain_any,
    back_any,
    filtered_a,
    filtered_b,
    smoothed_b,
    series,
    order,
    block,
    weight,
    filt_in,
    gain_in,
    back_in,
    info,
    half,
    quant,
    scale,
    land,
    scale_land,
    pair,
    ends,
    starts,
    carry,
    carry_land,
    filt,
    back,
    crossed,
    enter,
    gain,
    now,
    load,
    sib_send,
    sib_recv,
    info_send,
    info_recv,
    scale_send,
    scale_recv,
    carry_send,
    carry_recv,
):
    me = lax.axis_index("tm")
    core = lax.rem(me, 2)
    chip = lax.div(me, 2)
    sibling = me + 1 - 2 * core
    chips = devices // 2
    steps, columns = series.shape
    length = steps // devices
    states = filt_in.shape[0]
    span, gauges = weight.shape
    depth = length.bit_length() - 1
    scans = devices.bit_length() - 1
    halves = states // LANES

    loads = []
    for n, (source, target) in enumerate(
        (
            (filt_any, filt_in),
            (back_any, back_in),
            (order_any.at[me], order),
            (block_any, block),
            (weight_any, weight),
            (series_any, series),
            (gain_any, gain_in),
        )
    ):
        copy = pltpu.make_async_copy(source, target, load.at[n])
        copy.start()
        loads.append(copy)
    barrier = pltpu.get_barrier_semaphore()
    for k in range(1, devices):
        pl.semaphore_signal(
            barrier, inc=1, device_id={"tm": lax.rem(me + k, devices)}, device_id_type=MESH
        )

    def keep(ref, h, values):
        ref[h, 0], ref[h, 1] = split(values)

    def of(ref, h):
        return ref[h, 0], ref[h, 1]

    def power(h):
        for n, ref in enumerate((filt, back)):
            now[n] = 2.0 * now[n] - product(of(ref, h), of(ref, h))
            keep(ref, h + 1, now[n])

    def cross(h):
        now[3] = now[2] - product(of(enter, h), of(back, h))
        keep(crossed, h, now[3])

    def joined(h):
        now[2] = now[2] + now[3] - product(of(filt, h), of(crossed, h))
        keep(enter, h + 1, now[2])

    todo = []
    for k in range(max(2 * depth, depth + scans - 1)):
        if k < depth + scans - 1:
            todo.append((power, k))
        if k < 2 * depth:
            todo.append((joined if k % 2 else cross, k // 2))

    def advance(count=2):
        for work, h in todo[:count]:
            work(h)
        del todo[:count]

    loads[0].wait()
    loads[1].wait()
    now[0] = eye(states) - filt_in[...].T
    now[1] = eye(states) - back_in[...].T
    keep(filt, 0, now[0])
    keep(back, 0, now[1])
    now[2] = now[1] - product(of(filt, 0), of(back, 0))
    keep(enter, 0, now[2])
    advance()

    for copy in loads[2:]:
        copy.wait()
    number = order[...]
    upper = lax.div(number, WIDE)
    lower = lax.rem(number, WIDE)
    spot = lax.broadcasted_iota(jnp.int32, (WIDE, columns), 0)
    onehot = jnp.where(spot == lower, 1.0, 0.0).astype(jnp.bfloat16)
    parts = gauges // WIDE
    table = jnp.concatenate(
        [block[pl.ds(j, parts, stride=WIDE // LANES)] for j in range(WIDE // LANES)], 1
    )
    found = dot(table.astype(jnp.float32).astype(jnp.bfloat16), onehot)
    spot = lax.broadcasted_iota(jnp.int32, (parts, columns), 0)
    kind = jnp.sum(jnp.where(spot == upper, found, 0.0), 0, keepdims=True)
    weights = jnp.zeros((span, columns), jnp.float32)
    together = 8
    for base in range(0, parts, together):
        rows = [
            weight[:, (base + i) * WIDE : (base + i + 1) * WIDE]
            for i in range(min(together, parts - base))
        ]
        found = dot(jnp.concatenate(rows, 0), onehot)
        for i in range(len(rows)):
            weights = weights + jnp.where(
                upper == base + i, found[i * span : (i + 1) * span], 0.0
            )
        if base % (2 * together):
            advance()
    design = jnp.concatenate(
        [jnp.where(kind == float(k), weights, 0.0) for k in range(states // span)], 0
    ).astype(jnp.bfloat16)
    chunk = min(steps, 4 * length)
    for base in range(0, steps, chunk):
        partial = lax.dot_general(
            series[base : base + chunk],
            design,
            (((1,), (1,)), ((), ())),
            preferred_element_type=jnp.float32,
        )
        for b in range(base // length, (base + chunk) // length):
            row = b * length - base
            at = ((b % 2) * chips + b // 2) * length
            for j in range(halves):
                info[j, at : at + length] = partial[
                    row : row + length, j * LANES : (j + 1) * LANES
                ]
        if base == chunk:
            advance()
    pl.semaphore_wait(barrier, devices - 1)
    sib = []
    for t in range(chips):
        rows = pl.ds(pl.multiple_of(((1 - core) * chips + t) * length, length), length)
        copy = pltpu.make_async_remote_copy(
            src_ref=info.at[:, rows],
            dst_ref=half.at[t],
            send_sem=sib_send.at[t],
            recv_sem=sib_recv.at[t],
            device_id={"tm": sibling},
            device_id_type=MESH,
        )
        copy.start()
        sib.append(copy)
    tune = gain_in[...].T
    keep(gain, 0, tune)
    keep(gain, 2, tune - product(of(gain, 0), of(filt, 0)))
    tune = product(of(gain, 0), of(back, 0))
    keep(gain, 1, tune)
    keep(gain, 3, tune + product(of(gain, 0), of(crossed, 0)))
    keep(gain, 4, tune - product(of(gain, 1), of(back, 0)))
    advance(4)

    def summed(t):
        rows = pl.ds(pl.multiple_of(((1 - core) * chips + t) * length, length), length)
        pltpu.make_async_remote_copy(
            src_ref=info.at[:, rows],
            dst_ref=half.at[t],
            send_sem=sib_send.at[t],
            recv_sem=sib_recv.at[t],
            device_id={"tm": sibling},
            device_id_type=MESH,
        ).wait_recv()
        rows = pl.ds(pl.multiple_of((core * chips + t) * length, length), length)
        both = info[:, rows] + half[t]
        pair[:, pl.ds(pl.multiple_of(t * length, length), length)] = both
        return jnp.concatenate([both[j] for j in range(halves)], 1)

    sends = []

    def send(k, t, values):
        largest = jnp.maximum(jnp.max(jnp.abs(values), 0, keepdims=True), 1e-30)
        quant[k] = jnp.round(values * (LEVELS / largest)).astype(jnp.int32).astype(jnp.int16)
        scale[k] = largest * (1.0 / LEVELS)
        for source, target, sent, came in (
            (quant, land, info_send, info_recv),
            (scale, scale_land, scale_send, scale_recv),
        ):
            copy = pltpu.make_async_remote_copy(
                src_ref=source.at[k],
                dst_ref=target.at[chip],
                send_sem=sent.at[k],
                recv_sem=came.at[chip],
                device_id={"tm": 2 * t + core},
                device_id_type=MESH,
            )
            copy.start()
            sends.append(copy)

    for k in range(chips - 1):
        t = k + lax.div(k - chip + chips, chips)
        send(k, t, summed(t))
    total = summed(chip)

    for t in range(length):
        at = bit_reversed(t, depth) * chips
        for j in range(halves):
            ends[at : at + chips, j * LANES : (j + 1) * LANES] = pair[
                j, pl.ds(t, chips, stride=length)
            ]
    rows = chips * length // 2
    part = min(rows, 512)
    for base in range(0, rows, part):
        here = slice(base, base + part)
        left = split(ends[here])
        right = split(ends[rows + base : rows + base + part])
        starts[here] = product(left, of(gain, 3)) + product(right, of(gain, 4))
        ends[here] = product(left, of(gain, 2)) + product(right, of(gain, 0))
    advance()
    for h in range(1, depth):
        rows //= 2
        part = min(rows, 512)
        for base in range(0, rows, part):
            here = slice(base, base + part)
            there = slice(rows + base, rows + base + part)
            left = split(ends[here])
            starts[here] = (
                starts[here]
                + applied(starts[there], of(back, h))
                + product(left, of(crossed, h))
            )
            ends[here] = ends[there] + ends[here] - product(left, of(filt, h))
        advance()
    advance(len(todo))

    def spread(values):
        return jnp.concatenate(
            [
                jnp.where(core == b % 2, values[b // 2 : b // 2 + 1], 0.0)
                for b in range(devices)
            ],
            0,
        )

    reached = spread(ends[:chips])
    opened = spread(starts[:chips])
    for h in range(scans):
        reached = reached + applied(shift(reached, 1 << h), of(filt, depth + h))
    arrive = shift(reached, 1)
    final = reached[devices - 1 : devices]
    leaving = put_row(jnp.zeros_like(opened), final, devices - 1)
    opened = opened + matmul3(arrive, of(enter, depth)) + applied(leaving, of(back, depth))
    for h in range(scans):
        opened = opened + applied(shift(opened, -(1 << h)), of(back, depth + h))
    arrive_back = put_row(shift(opened, -1), final, devices - 1)
    for b in range(devices):
        carry[b, 0:1] = arrive[b : b + 1]
        carry[b, 1:2] = arrive_back[b : b + 1]

    carries = []
    for k in range(devices - 1):
        target = k + lax.div(k - me + devices, devices)
        copy = pltpu.make_async_remote_copy(
            src_ref=carry.at[target],
            dst_ref=carry_land.at[me],
            send_sem=carry_send.at[k],
            recv_sem=carry_recv.at[me],
            device_id={"tm": target},
            device_id_type=MESH,
        )
        copy.start()
        carries.append(copy)

    for k in range(chips - 1):
        s = k + lax.div(k - chip + chips, chips)
        for source, target, send, recv in (
            (quant, land, info_send, info_recv),
            (scale, scale_land, scale_send, scale_recv),
        ):
            pltpu.make_async_remote_copy(
                src_ref=source.at[k],
                dst_ref=target.at[s],
                send_sem=send.at[k],
                recv_sem=recv.at[s],
                device_id={"tm": 2 * s + core},
                device_id_type=MESH,
            ).wait_recv()
        total = total + land[s].astype(jnp.int32).astype(jnp.float32) * scale_land[s]
    ready = split(total)
    tails = [product(ready, of(gain, 0))]
    heads = [product(ready, of(gain, 1))]
    for h in range(depth - 1):
        inner = shift(tails[h], 1 - (1 << h)) if h else tails[h]
        heads.append(
            heads[h] + applied(shift(heads[h], -(1 << h)), of(back, h)) + matmul3(inner, of(crossed, h))
        )
        tails.append(tails[h] + applied(shift(tails[h], 1 << h), of(filt, h)))

    groups = length // GROUP

    def some(values, row):
        return jnp.concatenate(
            [values[n * GROUP + row : n * GROUP + row + 1] for n in range(groups)], 0
        )

    def down(before, after, h, reach, tail, head):
        offset = lax.rem(lax.broadcasted_iota(jnp.int32, before.shape, 0), 2 * reach)
        middle = shift(tail, 1) + applied(shift(before, reach), of(filt, h))
        before = jnp.where(offset == reach, middle, before)
        middle = head + matmul3(before, of(enter, h))
        middle = shift(middle, -1) + applied(shift(after, -reach), of(back, h))
        return before, jnp.where(offset == reach - 1, middle, after)

    small = GROUP.bit_length() - 1
    few = [(some(tails[h], GROUP - 1), some(heads[h], 0)) for h in range(small, depth)]
    entering = carry[me]
    for k in range(devices - 1):
        source = k + lax.div(k - me + devices, devices)
        pltpu.make_async_remote_copy(
            src_ref=carry.at[source],
            dst_ref=carry_land.at[source],
            send_sem=carry_send.at[k],
            recv_sem=carry_recv.at[source],
            device_id={"tm": source},
            device_id_type=MESH,
        ).wait_recv()
        entering = entering + carry_land[source]

    place = lax.broadcasted_iota(jnp.int32, (groups, states), 0)
    before = jnp.where(place == 0, entering[0:1], 0.0)
    after = jnp.where(place == groups - 1, entering[1:2], 0.0)
    for h in reversed(range(small, depth)):
        before, after = down(before, after, h, (1 << h) // GROUP, *few[h - small])
    before, after = (
        jnp.concatenate(
            [jnp.broadcast_to(rows[n : n + 1], (GROUP, states)) for n in range(groups)], 0
        )
        for rows in (before, after)
    )
    for h in reversed(range(small)):
        before, after = down(before, after, h, 1 << h, tails[h], heads[h])
    carried = applied(before, of(filt, 0))
    filtered_a[...] = tails[0]
    filtered_b[...] = carried
    smoothed_b[...] = heads[0] - tails[0] + matmul3(before, of(enter, 0)) + applied(after, of(back, 0))

    for copy in sib + sends + carries:
        copy.wait_send()


def per_device(
    gauge_series, gauge_order, gauge_block, gauge_weight, filt_trans, obs_gain, smooth_gain
):
    devices = lax.axis_size("tm")
    steps, columns = gauge_series.shape
    gauges, span = gauge_weight.shape
    states = filt_trans.shape[0]
    length = steps // devices
    chips = devices // 2
    depth = length.bit_length() - 1
    scans = devices.bit_length() - 1
    halves = states // LANES
    out = pltpu.VMEM((length, states), jnp.float32)
    square = (states, states)
    filtered_a, filtered_b, smoothed_b = pl.pallas_call(
        functools.partial(kernel, devices),
        out_shape=(out,) * 3,
        in_specs=[pl.BlockSpec(memory_space=pl.ANY)] * 7,
        out_specs=[pl.BlockSpec(memory_space=pltpu.VMEM)] * 3,
        scratch_shapes=[
            pltpu.VMEM((steps, columns), jnp.bfloat16),
            pltpu.VMEM((1, columns), jnp.int32),
            pltpu.VMEM((gauges // LANES, LANES), jnp.int32),
            pltpu.VMEM((span, gauges), jnp.bfloat16),
            pltpu.VMEM(square, jnp.float32),
            pltpu.VMEM(square, jnp.float32),
            pltpu.VMEM(square, jnp.float32),
            pltpu.VMEM((halves, steps, LANES), jnp.float32),
            pltpu.VMEM((chips, halves, length, LANES), jnp.float32),
            pltpu.VMEM((chips, length, states), jnp.int16),
            pltpu.VMEM((chips, 1, states), jnp.float32),
            pltpu.VMEM((chips, length, states), jnp.int16),
            pltpu.VMEM((chips, 1, states), jnp.float32),
            pltpu.VMEM((halves, chips * length, LANES), jnp.float32),
            pltpu.VMEM((chips * length, states), jnp.float32),
            pltpu.VMEM((chips * length, states), jnp.float32),
            pltpu.VMEM((devices, 2, states), jnp.float32),
            pltpu.VMEM((devices, 2, states), jnp.float32),
            pltpu.VMEM((depth + scans, 2) + square, jnp.bfloat16),
            pltpu.VMEM((depth + scans, 2) + square, jnp.bfloat16),
            pltpu.VMEM((depth, 2) + square, jnp.bfloat16),
            pltpu.VMEM((depth + 1, 2) + square, jnp.bfloat16),
            pltpu.VMEM((5, 2) + square, jnp.bfloat16),
            pltpu.VMEM((4,) + square, jnp.float32),
            pltpu.SemaphoreType.DMA((7,)),
            pltpu.SemaphoreType.DMA((chips,)),
            pltpu.SemaphoreType.DMA((chips,)),
            pltpu.SemaphoreType.DMA((chips,)),
            pltpu.SemaphoreType.DMA((chips,)),
            pltpu.SemaphoreType.DMA((chips,)),
            pltpu.SemaphoreType.DMA((chips,)),
            pltpu.SemaphoreType.DMA((devices,)),
            pltpu.SemaphoreType.DMA((devices,)),
        ],
        compiler_params=pltpu.CompilerParams(
            collective_id=0, has_side_effects=True, vmem_limit_bytes=58 << 20
        ),
    )(
        gauge_series,
        gauge_order.reshape(devices, 1, columns),
        gauge_block.reshape(-1, LANES),
        gauge_weight.T,
        filt_trans,
        obs_gain,
        smooth_gain,
    )
    return filtered_a + filtered_b, filtered_a + smoothed_b


def solution(mesh):
    placed = (
        P("groups", "tm"),
        P(),
        P(),
        P(),
        P("groups", None),
        P("groups", None),
        P("groups", None),
    )
    return jax.shard_map(
        per_device,
        mesh=mesh,
        in_specs=placed,
        out_specs=(P(("groups", "tm"), None), P(("groups", "tm"), None)),
        check_vma=False,
    )
```

```python
import functools

import jax
import jax.numpy as jnp
from jax import lax
from jax.experimental import pallas as pl
from jax.experimental.pallas import tpu as pltpu
from jax.sharding import PartitionSpec as P

MESH = pl.DeviceIdType.MESH
LANES = 128
WIDE = 256
LEVELS = 32704.0
GROUP = 8


def dot(left, right):
    return jnp.dot(left, right, preferred_element_type=jnp.float32)


def split(values):
    high = values.astype(jnp.bfloat16)
    return high, (values - high.astype(jnp.float32)).astype(jnp.bfloat16)


def product(left, right):
    high, low = left
    top, rest = right
    rows = high.shape[0]
    both = dot(jnp.concatenate([high, low], 0), top)
    return dot(high, rest) + both[:rows] + both[rows:]


def matmul3(left, right):
    return product(split(left), right)


def applied(values, right):
    return values - matmul3(values, right)


def eye(size):
    row = lax.broadcasted_iota(jnp.int32, (size, size), 0)
    column = lax.broadcasted_iota(jnp.int32, (size, size), 1)
    return jnp.where(row == column, 1.0, 0.0)


def shift(values, offset):
    rows = values.shape[0]
    moved = pltpu.roll(values, offset % rows, 0)
    place = lax.broadcasted_iota(jnp.int32, values.shape, 0)
    kept = place >= offset if offset > 0 else place < rows + offset
    return jnp.where(kept, moved, 0.0)


def put_row(values, row, where):
    place = lax.broadcasted_iota(jnp.int32, values.shape, 0)
    return values + jnp.where(place == where, row, 0.0)


def bit_reversed(number, bits):
    return int(format(number, "b").zfill(bits)[::-1], 2) if bits else 0


def kernel(
    devices,
    series_any,
    order_any,
    block_any,
    weight_any,
    filt_any,
    gain_any,
    back_any,
    filtered_a,
    filtered_b,
    smoothed_b,
    series,
    order,
    block,
    weight,
    filt_in,
    gain_in,
    back_in,
    info,
    half,
    quant,
    scale,
    land,
    scale_land,
    pair,
    ends,
    starts,
    carry,
    carry_land,
    filt,
    back,
    crossed,
    enter,
    gain,
    now,
    load,
    sib_send,
    sib_recv,
    info_send,
    info_recv,
    scale_send,
    scale_recv,
    carry_send,
    carry_recv,
):
    me = lax.axis_index("tm")
    core = lax.rem(me, 2)
    chip = lax.div(me, 2)
    sibling = me + 1 - 2 * core
    chips = devices // 2
    steps, columns = series.shape
    length = steps // devices
    states = filt_in.shape[0]
    span, gauges = weight.shape
    depth = length.bit_length() - 1
    scans = devices.bit_length() - 1
    halves = states // LANES

    loads = []
    for n, (source, target) in enumerate(
        (
            (filt_any, filt_in),
            (back_any, back_in),
            (order_any.at[me], order),
            (block_any, block),
            (weight_any, weight),
            (series_any, series),
            (gain_any, gain_in),
        )
    ):
        copy = pltpu.make_async_copy(source, target, load.at[n])
        copy.start()
        loads.append(copy)
    barrier = pltpu.get_barrier_semaphore()
    for k in range(1, devices):
        pl.semaphore_signal(
            barrier, inc=1, device_id={"tm": lax.rem(me + k, devices)}, device_id_type=MESH
        )

    def keep(ref, h, values):
        ref[h, 0], ref[h, 1] = split(values)

    def of(ref, h):
        return ref[h, 0], ref[h, 1]

    def power(h):
        for n, ref in enumerate((filt, back)):
            now[n] = 2.0 * now[n] - product(of(ref, h), of(ref, h))
            keep(ref, h + 1, now[n])

    def cross(h):
        now[3] = now[2] - product(of(enter, h), of(back, h))
        keep(crossed, h, now[3])

    def joined(h):
        now[2] = now[2] + now[3] - product(of(filt, h), of(crossed, h))
        keep(enter, h + 1, now[2])

    todo = []
    for k in range(max(2 * depth, depth + scans - 1)):
        if k < depth + scans - 1:
            todo.append((power, k))
        if k < 2 * depth:
            todo.append((joined if k % 2 else cross, k // 2))

    def advance(count=2):
        for work, h in todo[:count]:
            work(h)
        del todo[:count]

    loads[0].wait()
    loads[1].wait()
    now[0] = eye(states) - filt_in[...].T
    now[1] = eye(states) - back_in[...].T
    keep(filt, 0, now[0])
    keep(back, 0, now[1])
    now[2] = now[1] - product(of(filt, 0), of(back, 0))
    keep(enter, 0, now[2])
    advance()

    for copy in loads[2:]:
        copy.wait()
    number = order[...]
    upper = lax.div(number, WIDE)
    lower = lax.rem(number, WIDE)
    spot = lax.broadcasted_iota(jnp.int32, (WIDE, columns), 0)
    onehot = jnp.where(spot == lower, 1.0, 0.0).astype(jnp.bfloat16)
    parts = gauges // WIDE
    table = jnp.concatenate(
        [block[pl.ds(j, parts, stride=WIDE // LANES)] for j in range(WIDE // LANES)], 1
    )
    found = dot(table.astype(jnp.float32).astype(jnp.bfloat16), onehot)
    spot = lax.broadcasted_iota(jnp.int32, (parts, columns), 0)
    kind = jnp.sum(jnp.where(spot == upper, found, 0.0), 0, keepdims=True)
    weights = jnp.zeros((span, columns), jnp.float32)
    together = 8
    for base in range(0, parts, together):
        rows = [
            weight[:, (base + i) * WIDE : (base + i + 1) * WIDE]
            for i in range(min(together, parts - base))
        ]
        found = dot(jnp.concatenate(rows, 0), onehot)
        for i in range(len(rows)):
            weights = weights + jnp.where(
                upper == base + i, found[i * span : (i + 1) * span], 0.0
            )
        if base % (2 * together):
            advance()
    design = jnp.concatenate(
        [jnp.where(kind == float(k), weights, 0.0) for k in range(states // span)], 0
    ).astype(jnp.bfloat16)
    chunk = min(steps, 4 * length)
    for base in range(0, steps, chunk):
        partial = lax.dot_general(
            series[base : base + chunk],
            design,
            (((1,), (1,)), ((), ())),
            preferred_element_type=jnp.float32,
        )
        for b in range(base // length, (base + chunk) // length):
            row = b * length - base
            at = ((b % 2) * chips + b // 2) * length
            for j in range(halves):
                info[j, at : at + length] = partial[
                    row : row + length, j * LANES : (j + 1) * LANES
                ]
        if base == chunk:
            advance()
    pl.semaphore_wait(barrier, devices - 1)
    sib = []
    for t in range(chips):
        rows = pl.ds(pl.multiple_of(((1 - core) * chips + t) * length, length), length)
        copy = pltpu.make_async_remote_copy(
            src_ref=info.at[:, rows],
            dst_ref=half.at[t],
            send_sem=sib_send.at[t],
            recv_sem=sib_recv.at[t],
            device_id={"tm": sibling},
            device_id_type=MESH,
        )
        copy.start()
        sib.append(copy)
    tune = gain_in[...].T
    keep(gain, 0, tune)
    advance()
    keep(gain, 2, tune - product(of(gain, 0), of(filt, 0)))
    tune = product(of(gain, 0), of(back, 0))
    keep(gain, 1, tune)
    keep(gain, 3, tune + product(of(gain, 0), of(crossed, 0)))
    keep(gain, 4, tune - product(of(gain, 1), of(back, 0)))
    advance()

    def summed(t):
        rows = pl.ds(pl.multiple_of(((1 - core) * chips + t) * length, length), length)
        pltpu.make_async_remote_copy(
            src_ref=info.at[:, rows],
            dst_ref=half.at[t],
            send_sem=sib_send.at[t],
            recv_sem=sib_recv.at[t],
            device_id={"tm": sibling},
            device_id_type=MESH,
        ).wait_recv()
        rows = pl.ds(pl.multiple_of((core * chips + t) * length, length), length)
        both = info[:, rows] + half[t]
        pair[:, pl.ds(pl.multiple_of(t * length, length), length)] = both
        return jnp.concatenate([both[j] for j in range(halves)], 1)

    sends = []

    def send(k, t, values):
        largest = jnp.maximum(jnp.max(jnp.abs(values), 0, keepdims=True), 1e-30)
        quant[k] = jnp.round(values * (LEVELS / largest)).astype(jnp.int32).astype(jnp.int16)
        scale[k] = largest * (1.0 / LEVELS)
        for source, target, sent, came in (
            (quant, land, info_send, info_recv),
            (scale, scale_land, scale_send, scale_recv),
        ):
            copy = pltpu.make_async_remote_copy(
                src_ref=source.at[k],
                dst_ref=target.at[chip],
                send_sem=sent.at[k],
                recv_sem=came.at[chip],
                device_id={"tm": 2 * t + core},
                device_id_type=MESH,
            )
            copy.start()
            sends.append(copy)

    for k in range(chips - 1):
        t = k + lax.div(k - chip + chips, chips)
        send(k, t, summed(t))
    total = summed(chip)

    for t in range(length):
        at = bit_reversed(t, depth) * chips
        for j in range(halves):
            ends[at : at + chips, j * LANES : (j + 1) * LANES] = pair[
                j, pl.ds(t, chips, stride=length)
            ]
    rows = chips * length // 2
    part = min(rows, 512)
    for base in range(0, rows, part):
        here = slice(base, base + part)
        left = split(ends[here])
        right = split(ends[rows + base : rows + base + part])
        starts[here] = product(left, of(gain, 3)) + product(right, of(gain, 4))
        ends[here] = product(left, of(gain, 2)) + product(right, of(gain, 0))
    advance()
    for h in range(1, depth):
        rows //= 2
        part = min(rows, 512)
        for base in range(0, rows, part):
            here = slice(base, base + part)
            there = slice(rows + base, rows + base + part)
            left = split(ends[here])
            starts[here] = (
                starts[here]
                + applied(starts[there], of(back, h))
                + product(left, of(crossed, h))
            )
            ends[here] = ends[there] + ends[here] - product(left, of(filt, h))
        advance()
    advance(len(todo))

    def spread(values):
        return jnp.concatenate(
            [
                jnp.where(core == b % 2, values[b // 2 : b // 2 + 1], 0.0)
                for b in range(devices)
            ],
            0,
        )

    reached = spread(ends[:chips])
    opened = spread(starts[:chips])
    for h in range(scans):
        reached = reached + applied(shift(reached, 1 << h), of(filt, depth + h))
    arrive = shift(reached, 1)
    final = reached[devices - 1 : devices]
    leaving = put_row(jnp.zeros_like(opened), final, devices - 1)
    opened = opened + matmul3(arrive, of(enter, depth)) + applied(leaving, of(back, depth))
    for h in range(scans):
        opened = opened + applied(shift(opened, -(1 << h)), of(back, depth + h))
    arrive_back = put_row(shift(opened, -1), final, devices - 1)
    for b in range(devices):
        carry[b, 0:1] = arrive[b : b + 1]
        carry[b, 1:2] = arrive_back[b : b + 1]

    carries = []
    for k in range(devices - 1):
        target = k + lax.div(k - me + devices, devices)
        copy = pltpu.make_async_remote_copy(
            src_ref=carry.at[target],
            dst_ref=carry_land.at[me],
            send_sem=carry_send.at[k],
            recv_sem=carry_recv.at[me],
            device_id={"tm": target},
            device_id_type=MESH,
        )
        copy.start()
        carries.append(copy)

    for k in range(chips - 1):
        s = k + lax.div(k - chip + chips, chips)
        for source, target, send, recv in (
            (quant, land, info_send, info_recv),
            (scale, scale_land, scale_send, scale_recv),
        ):
            pltpu.make_async_remote_copy(
                src_ref=source.at[k],
                dst_ref=target.at[s],
                send_sem=send.at[k],
                recv_sem=recv.at[s],
                device_id={"tm": 2 * s + core},
                device_id_type=MESH,
            ).wait_recv()
        total = total + land[s].astype(jnp.int32).astype(jnp.float32) * scale_land[s]
    ready = split(total)
    tails = [product(ready, of(gain, 0))]
    heads = [product(ready, of(gain, 1))]
    for h in range(depth - 1):
        inner = shift(tails[h], 1 - (1 << h)) if h else tails[h]
        heads.append(
            heads[h] + applied(shift(heads[h], -(1 << h)), of(back, h)) + matmul3(inner, of(crossed, h))
        )
        tails.append(tails[h] + applied(shift(tails[h], 1 << h), of(filt, h)))

    groups = length // GROUP

    def some(values, row):
        return jnp.concatenate(
            [values[n * GROUP + row : n * GROUP + row + 1] for n in range(groups)], 0
        )

    def down(before, after, h, reach, tail, head):
        offset = lax.rem(lax.broadcasted_iota(jnp.int32, before.shape, 0), 2 * reach)
        middle = shift(tail, 1) + applied(shift(before, reach), of(filt, h))
        before = jnp.where(offset == reach, middle, before)
        middle = head + matmul3(before, of(enter, h))
        middle = shift(middle, -1) + applied(shift(after, -reach), of(back, h))
        return before, jnp.where(offset == reach - 1, middle, after)

    small = GROUP.bit_length() - 1
    few = [(some(tails[h], GROUP - 1), some(heads[h], 0)) for h in range(small, depth)]
    entering = carry[me]
    for k in range(devices - 1):
        source = k + lax.div(k - me + devices, devices)
        pltpu.make_async_remote_copy(
            src_ref=carry.at[source],
            dst_ref=carry_land.at[source],
            send_sem=carry_send.at[k],
            recv_sem=carry_recv.at[source],
            device_id={"tm": source},
            device_id_type=MESH,
        ).wait_recv()
        entering = entering + carry_land[source]

    place = lax.broadcasted_iota(jnp.int32, (groups, states), 0)
    before = jnp.where(place == 0, entering[0:1], 0.0)
    after = jnp.where(place == groups - 1, entering[1:2], 0.0)
    for h in reversed(range(small, depth)):
        before, after = down(before, after, h, (1 << h) // GROUP, *few[h - small])
    before, after = (
        jnp.concatenate(
            [jnp.broadcast_to(rows[n : n + 1], (GROUP, states)) for n in range(groups)], 0
        )
        for rows in (before, after)
    )
    for h in reversed(range(small)):
        before, after = down(before, after, h, 1 << h, tails[h], heads[h])
    carried = applied(before, of(filt, 0))
    filtered_a[...] = tails[0]
    filtered_b[...] = carried
    smoothed_b[...] = heads[0] - tails[0] + matmul3(before, of(enter, 0)) + applied(after, of(back, 0))

    for copy in sib + sends + carries:
        copy.wait_send()


def per_device(
    gauge_series, gauge_order, gauge_block, gauge_weight, filt_trans, obs_gain, smooth_gain
):
    devices = lax.axis_size("tm")
    steps, columns = gauge_series.shape
    gauges, span = gauge_weight.shape
    states = filt_trans.shape[0]
    length = steps // devices
    chips = devices // 2
    depth = length.bit_length() - 1
    scans = devices.bit_length() - 1
    halves = states // LANES
    out = pltpu.VMEM((length, states), jnp.float32)
    square = (states, states)
    filtered_a, filtered_b, smoothed_b = pl.pallas_call(
        functools.partial(kernel, devices),
        out_shape=(out,) * 3,
        in_specs=[pl.BlockSpec(memory_space=pl.ANY)] * 7,
        out_specs=[pl.BlockSpec(memory_space=pltpu.VMEM)] * 3,
        scratch_shapes=[
            pltpu.VMEM((steps, columns), jnp.bfloat16),
            pltpu.VMEM((1, columns), jnp.int32),
            pltpu.VMEM((gauges // LANES, LANES), jnp.int32),
            pltpu.VMEM((span, gauges), jnp.bfloat16),
            pltpu.VMEM(square, jnp.float32),
            pltpu.VMEM(square, jnp.float32),
            pltpu.VMEM(square, jnp.float32),
            pltpu.VMEM((halves, steps, LANES), jnp.float32),
            pltpu.VMEM((chips, halves, length, LANES), jnp.float32),
            pltpu.VMEM((chips, length, states), jnp.int16),
            pltpu.VMEM((chips, 1, states), jnp.float32),
            pltpu.VMEM((chips, length, states), jnp.int16),
            pltpu.VMEM((chips, 1, states), jnp.float32),
            pltpu.VMEM((halves, chips * length, LANES), jnp.float32),
            pltpu.VMEM((chips * length, states), jnp.float32),
            pltpu.VMEM((chips * length, states), jnp.float32),
            pltpu.VMEM((devices, 2, states), jnp.float32),
            pltpu.VMEM((devices, 2, states), jnp.float32),
            pltpu.VMEM((depth + scans, 2) + square, jnp.bfloat16),
            pltpu.VMEM((depth + scans, 2) + square, jnp.bfloat16),
            pltpu.VMEM((depth, 2) + square, jnp.bfloat16),
            pltpu.VMEM((depth + 1, 2) + square, jnp.bfloat16),
            pltpu.VMEM((5, 2) + square, jnp.bfloat16),
            pltpu.VMEM((4,) + square, jnp.float32),
            pltpu.SemaphoreType.DMA((7,)),
            pltpu.SemaphoreType.DMA((chips,)),
            pltpu.SemaphoreType.DMA((chips,)),
            pltpu.SemaphoreType.DMA((chips,)),
            pltpu.SemaphoreType.DMA((chips,)),
            pltpu.SemaphoreType.DMA((chips,)),
            pltpu.SemaphoreType.DMA((chips,)),
            pltpu.SemaphoreType.DMA((devices,)),
            pltpu.SemaphoreType.DMA((devices,)),
        ],
        compiler_params=pltpu.CompilerParams(
            collective_id=0, has_side_effects=True, vmem_limit_bytes=58 << 20
        ),
    )(
        gauge_series,
        gauge_order.reshape(devices, 1, columns),
        gauge_block.reshape(-1, LANES),
        gauge_weight.T,
        filt_trans,
        obs_gain,
        smooth_gain,
    )
    return filtered_a + filtered_b, filtered_a + smoothed_b


def solution(mesh):
    placed = (
        P("groups", "tm"),
        P(),
        P(),
        P(),
        P("groups", None),
        P("groups", None),
        P("groups", None),
    )
    return jax.shard_map(
        per_device,
        mesh=mesh,
        in_specs=placed,
        out_specs=(P(("groups", "tm"), None), P(("groups", "tm"), None)),
        check_vma=False,
    )
```

```python
import functools

import jax
import jax.numpy as jnp
from jax import lax
from jax.experimental import pallas as pl
from jax.experimental.pallas import tpu as pltpu
from jax.sharding import PartitionSpec as P

MESH = pl.DeviceIdType.MESH
LANES = 128
WIDE = 256
LEVELS = 32704.0
GROUP = 8


def dot(left, right):
    return jnp.dot(left, right, preferred_element_type=jnp.float32)


def split(values):
    high = values.astype(jnp.bfloat16)
    return high, (values - high.astype(jnp.float32)).astype(jnp.bfloat16)


def product(left, right):
    high, low = left
    top, rest = right
    rows = high.shape[0]
    both = dot(jnp.concatenate([high, low], 0), top)
    return dot(high, rest) + both[:rows] + both[rows:]


def matmul3(left, right):
    return product(split(left), right)


def applied(values, right):
    return values - matmul3(values, right)


def eye(size):
    row = lax.broadcasted_iota(jnp.int32, (size, size), 0)
    column = lax.broadcasted_iota(jnp.int32, (size, size), 1)
    return jnp.where(row == column, 1.0, 0.0)


def shift(values, offset):
    rows = values.shape[0]
    moved = pltpu.roll(values, offset % rows, 0)
    place = lax.broadcasted_iota(jnp.int32, values.shape, 0)
    kept = place >= offset if offset > 0 else place < rows + offset
    return jnp.where(kept, moved, 0.0)


def put_row(values, row, where):
    place = lax.broadcasted_iota(jnp.int32, values.shape, 0)
    return values + jnp.where(place == where, row, 0.0)


def bit_reversed(number, bits):
    return int(format(number, "b").zfill(bits)[::-1], 2) if bits else 0


def kernel(
    devices,
    series_any,
    order_any,
    block_any,
    weight_any,
    filt_any,
    gain_any,
    back_any,
    filtered_a,
    filtered_b,
    smoothed_b,
    series,
    order,
    block,
    weight,
    filt_in,
    gain_in,
    back_in,
    info,
    half,
    quant,
    scale,
    land,
    scale_land,
    pair,
    ends,
    starts,
    carry,
    carry_land,
    filt,
    back,
    crossed,
    enter,
    gain,
    now,
    load,
    sib_send,
    sib_recv,
    info_send,
    info_recv,
    scale_send,
    scale_recv,
    carry_send,
    carry_recv,
):
    me = lax.axis_index("tm")
    core = lax.rem(me, 2)
    chip = lax.div(me, 2)
    sibling = me + 1 - 2 * core
    chips = devices // 2
    steps, columns = series.shape
    length = steps // devices
    states = filt_in.shape[0]
    span, gauges = weight.shape
    depth = length.bit_length() - 1
    scans = devices.bit_length() - 1
    halves = states // LANES

    loads = []
    for n, (source, target) in enumerate(
        (
            (filt_any, filt_in),
            (back_any, back_in),
            (order_any.at[me], order),
            (block_any, block),
            (weight_any, weight),
            (series_any, series),
            (gain_any, gain_in),
        )
    ):
        copy = pltpu.make_async_copy(source, target, load.at[n])
        copy.start()
        loads.append(copy)
    barrier = pltpu.get_barrier_semaphore()
    for k in range(1, devices):
        pl.semaphore_signal(
            barrier, inc=1, device_id={"tm": lax.rem(me + k, devices)}, device_id_type=MESH
        )

    def keep(ref, h, values):
        ref[h, 0], ref[h, 1] = split(values)

    def of(ref, h):
        return ref[h, 0], ref[h, 1]

    def power(h):
        for n, ref in enumerate((filt, back)):
            now[n] = 2.0 * now[n] - product(of(ref, h), of(ref, h))
            keep(ref, h + 1, now[n])

    def cross(h):
        now[3] = now[2] - product(of(enter, h), of(back, h))
        keep(crossed, h, now[3])

    def joined(h):
        now[2] = now[2] + now[3] - product(of(filt, h), of(crossed, h))
        keep(enter, h + 1, now[2])

    todo = []
    for k in range(max(2 * depth, depth + scans - 1)):
        if k < depth + scans - 1:
            todo.append((power, k))
        if k < 2 * depth:
            todo.append((joined if k % 2 else cross, k // 2))

    def advance(count=2):
        for work, h in todo[:count]:
            work(h)
        del todo[:count]

    loads[0].wait()
    loads[1].wait()
    now[0] = eye(states) - filt_in[...].T
    now[1] = eye(states) - back_in[...].T
    keep(filt, 0, now[0])
    keep(back, 0, now[1])
    now[2] = now[1] - product(of(filt, 0), of(back, 0))
    keep(enter, 0, now[2])
    advance()

    for copy in loads[2:]:
        copy.wait()
    number = order[...]
    upper = lax.div(number, WIDE)
    lower = lax.rem(number, WIDE)
    spot = lax.broadcasted_iota(jnp.int32, (WIDE, columns), 0)
    onehot = jnp.where(spot == lower, 1.0, 0.0).astype(jnp.bfloat16)
    parts = gauges // WIDE
    table = jnp.concatenate(
        [block[pl.ds(j, parts, stride=WIDE // LANES)] for j in range(WIDE // LANES)], 1
    )
    found = dot(table.astype(jnp.float32).astype(jnp.bfloat16), onehot)
    spot = lax.broadcasted_iota(jnp.int32, (parts, columns), 0)
    kind = jnp.sum(jnp.where(spot == upper, found, 0.0), 0, keepdims=True)
    weights = jnp.zeros((span, columns), jnp.float32)
    together = 8
    for base in range(0, parts, together):
        rows = [
            weight[:, (base + i) * WIDE : (base + i + 1) * WIDE]
            for i in range(min(together, parts - base))
        ]
        found = dot(jnp.concatenate(rows, 0), onehot)
        for i in range(len(rows)):
            weights = weights + jnp.where(
                upper == base + i, found[i * span : (i + 1) * span], 0.0
            )
        if base % (2 * together):
            advance()
    design = jnp.concatenate(
        [jnp.where(kind == float(k), weights, 0.0) for k in range(states // span)], 0
    ).astype(jnp.bfloat16)
    chunk = min(steps, 4 * length)
    for base in range(0, steps, chunk):
        partial = lax.dot_general(
            series[base : base + chunk],
            design,
            (((1,), (1,)), ((), ())),
            preferred_element_type=jnp.float32,
        )
        for b in range(base // length, (base + chunk) // length):
            row = b * length - base
            at = ((b % 2) * chips + b // 2) * length
            for j in range(halves):
                info[j, at : at + length] = partial[
                    row : row + length, j * LANES : (j + 1) * LANES
                ]
        if base == chunk:
            advance()
    pl.semaphore_wait(barrier, devices - 1)
    sib = []
    for t in range(chips):
        rows = pl.ds(pl.multiple_of(((1 - core) * chips + t) * length, length), length)
        copy = pltpu.make_async_remote_copy(
            src_ref=info.at[:, rows],
            dst_ref=half.at[t],
            send_sem=sib_send.at[t],
            recv_sem=sib_recv.at[t],
            device_id={"tm": sibling},
            device_id_type=MESH,
        )
        copy.start()
        sib.append(copy)
    tune = gain_in[...].T
    keep(gain, 0, tune)
    keep(gain, 2, tune - product(of(gain, 0), of(filt, 0)))
    tune = product(of(gain, 0), of(back, 0))
    keep(gain, 1, tune)
    keep(gain, 3, tune + product(of(gain, 0), of(crossed, 0)))
    keep(gain, 4, tune - product(of(gain, 1), of(back, 0)))
    advance(3)

    def summed(t):
        rows = pl.ds(pl.multiple_of(((1 - core) * chips + t) * length, length), length)
        pltpu.make_async_remote_copy(
            src_ref=info.at[:, rows],
            dst_ref=half.at[t],
            send_sem=sib_send.at[t],
            recv_sem=sib_recv.at[t],
            device_id={"tm": sibling},
            device_id_type=MESH,
        ).wait_recv()
        rows = pl.ds(pl.multiple_of((core * chips + t) * length, length), length)
        both = info[:, rows] + half[t]
        pair[:, pl.ds(pl.multiple_of(t * length, length), length)] = both
        return jnp.concatenate([both[j] for j in range(halves)], 1)

    sends = []

    def send(k, t, values):
        largest = jnp.maximum(jnp.max(jnp.abs(values), 0, keepdims=True), 1e-30)
        quant[k] = jnp.round(values * (LEVELS / largest)).astype(jnp.int32).astype(jnp.int16)
        scale[k] = largest * (1.0 / LEVELS)
        for source, target, sent, came in (
            (quant, land, info_send, info_recv),
            (scale, scale_land, scale_send, scale_recv),
        ):
            copy = pltpu.make_async_remote_copy(
                src_ref=source.at[k],
                dst_ref=target.at[chip],
                send_sem=sent.at[k],
                recv_sem=came.at[chip],
                device_id={"tm": 2 * t + core},
                device_id_type=MESH,
            )
            copy.start()
            sends.append(copy)

    for k in range(chips - 1):
        t = k + lax.div(k - chip + chips, chips)
        send(k, t, summed(t))
    total = summed(chip)
    advance(1)

    for t in range(length):
        at = bit_reversed(t, depth) * chips
        for j in range(halves):
            ends[at : at + chips, j * LANES : (j + 1) * LANES] = pair[
                j, pl.ds(t, chips, stride=length)
            ]
    rows = chips * length // 2
    part = min(rows, 512)
    for base in range(0, rows, part):
        here = slice(base, base + part)
        left = split(ends[here])
        right = split(ends[rows + base : rows + base + part])
        starts[here] = product(left, of(gain, 3)) + product(right, of(gain, 4))
        ends[here] = product(left, of(gain, 2)) + product(right, of(gain, 0))
    advance()
    for h in range(1, depth):
        rows //= 2
        part = min(rows, 512)
        for base in range(0, rows, part):
            here = slice(base, base + part)
            there = slice(rows + base, rows + base + part)
            left = split(ends[here])
            starts[here] = (
                starts[here]
                + applied(starts[there], of(back, h))
                + product(left, of(crossed, h))
            )
            ends[here] = ends[there] + ends[here] - product(left, of(filt, h))
        advance()
    advance(len(todo))

    def spread(values):
        return jnp.concatenate(
            [
                jnp.where(core == b % 2, values[b // 2 : b // 2 + 1], 0.0)
                for b in range(devices)
            ],
            0,
        )

    reached = spread(ends[:chips])
    opened = spread(starts[:chips])
    for h in range(scans):
        reached = reached + applied(shift(reached, 1 << h), of(filt, depth + h))
    arrive = shift(reached, 1)
    final = reached[devices - 1 : devices]
    leaving = put_row(jnp.zeros_like(opened), final, devices - 1)
    opened = opened + matmul3(arrive, of(enter, depth)) + applied(leaving, of(back, depth))
    for h in range(scans):
        opened = opened + applied(shift(opened, -(1 << h)), of(back, depth + h))
    arrive_back = put_row(shift(opened, -1), final, devices - 1)
    for b in range(devices):
        carry[b, 0:1] = arrive[b : b + 1]
        carry[b, 1:2] = arrive_back[b : b + 1]

    carries = []
    for k in range(devices - 1):
        target = k + lax.div(k - me + devices, devices)
        copy = pltpu.make_async_remote_copy(
            src_ref=carry.at[target],
            dst_ref=carry_land.at[me],
            send_sem=carry_send.at[k],
            recv_sem=carry_recv.at[me],
            device_id={"tm": target},
            device_id_type=MESH,
        )
        copy.start()
        carries.append(copy)

    for k in range(chips - 1):
        s = k + lax.div(k - chip + chips, chips)
        for source, target, send, recv in (
            (quant, land, info_send, info_recv),
            (scale, scale_land, scale_send, scale_recv),
        ):
            pltpu.make_async_remote_copy(
                src_ref=source.at[k],
                dst_ref=target.at[s],
                send_sem=send.at[k],
                recv_sem=recv.at[s],
                device_id={"tm": 2 * s + core},
                device_id_type=MESH,
            ).wait_recv()
        total = total + land[s].astype(jnp.int32).astype(jnp.float32) * scale_land[s]
    ready = split(total)
    tails = [product(ready, of(gain, 0))]
    heads = [product(ready, of(gain, 1))]
    for h in range(depth - 1):
        inner = shift(tails[h], 1 - (1 << h)) if h else tails[h]
        heads.append(
            heads[h] + applied(shift(heads[h], -(1 << h)), of(back, h)) + matmul3(inner, of(crossed, h))
        )
        tails.append(tails[h] + applied(shift(tails[h], 1 << h), of(filt, h)))

    groups = length // GROUP

    def some(values, row):
        return jnp.concatenate(
            [values[n * GROUP + row : n * GROUP + row + 1] for n in range(groups)], 0
        )

    def down(before, after, h, reach, tail, head):
        offset = lax.rem(lax.broadcasted_iota(jnp.int32, before.shape, 0), 2 * reach)
        middle = shift(tail, 1) + applied(shift(before, reach), of(filt, h))
        before = jnp.where(offset == reach, middle, before)
        middle = head + matmul3(before, of(enter, h))
        middle = shift(middle, -1) + applied(shift(after, -reach), of(back, h))
        return before, jnp.where(offset == reach - 1, middle, after)

    small = GROUP.bit_length() - 1
    few = [(some(tails[h], GROUP - 1), some(heads[h], 0)) for h in range(small, depth)]
    entering = carry[me]
    for k in range(devices - 1):
        source = k + lax.div(k - me + devices, devices)
        pltpu.make_async_remote_copy(
            src_ref=carry.at[source],
            dst_ref=carry_land.at[source],
            send_sem=carry_send.at[k],
            recv_sem=carry_recv.at[source],
            device_id={"tm": source},
            device_id_type=MESH,
        ).wait_recv()
        entering = entering + carry_land[source]

    place = lax.broadcasted_iota(jnp.int32, (groups, states), 0)
    before = jnp.where(place == 0, entering[0:1], 0.0)
    after = jnp.where(place == groups - 1, entering[1:2], 0.0)
    for h in reversed(range(small, depth)):
        before, after = down(before, after, h, (1 << h) // GROUP, *few[h - small])
    before, after = (
        jnp.concatenate(
            [jnp.broadcast_to(rows[n : n + 1], (GROUP, states)) for n in range(groups)], 0
        )
        for rows in (before, after)
    )
    for h in reversed(range(small)):
        before, after = down(before, after, h, 1 << h, tails[h], heads[h])
    carried = applied(before, of(filt, 0))
    filtered_a[...] = tails[0]
    filtered_b[...] = carried
    smoothed_b[...] = heads[0] - tails[0] + matmul3(before, of(enter, 0)) + applied(after, of(back, 0))

    for copy in sib + sends + carries:
        copy.wait_send()


def per_device(
    gauge_series, gauge_order, gauge_block, gauge_weight, filt_trans, obs_gain, smooth_gain
):
    devices = lax.axis_size("tm")
    steps, columns = gauge_series.shape
    gauges, span = gauge_weight.shape
    states = filt_trans.shape[0]
    length = steps // devices
    chips = devices // 2
    depth = length.bit_length() - 1
    scans = devices.bit_length() - 1
    halves = states // LANES
    out = pltpu.VMEM((length, states), jnp.float32)
    square = (states, states)
    filtered_a, filtered_b, smoothed_b = pl.pallas_call(
        functools.partial(kernel, devices),
        out_shape=(out,) * 3,
        in_specs=[pl.BlockSpec(memory_space=pl.ANY)] * 7,
        out_specs=[pl.BlockSpec(memory_space=pltpu.VMEM)] * 3,
        scratch_shapes=[
            pltpu.VMEM((steps, columns), jnp.bfloat16),
            pltpu.VMEM((1, columns), jnp.int32),
            pltpu.VMEM((gauges // LANES, LANES), jnp.int32),
            pltpu.VMEM((span, gauges), jnp.bfloat16),
            pltpu.VMEM(square, jnp.float32),
            pltpu.VMEM(square, jnp.float32),
            pltpu.VMEM(square, jnp.float32),
            pltpu.VMEM((halves, steps, LANES), jnp.float32),
            pltpu.VMEM((chips, halves, length, LANES), jnp.float32),
            pltpu.VMEM((chips, length, states), jnp.int16),
            pltpu.VMEM((chips, 1, states), jnp.float32),
            pltpu.VMEM((chips, length, states), jnp.int16),
            pltpu.VMEM((chips, 1, states), jnp.float32),
            pltpu.VMEM((halves, chips * length, LANES), jnp.float32),
            pltpu.VMEM((chips * length, states), jnp.float32),
            pltpu.VMEM((chips * length, states), jnp.float32),
            pltpu.VMEM((devices, 2, states), jnp.float32),
            pltpu.VMEM((devices, 2, states), jnp.float32),
            pltpu.VMEM((depth + scans, 2) + square, jnp.bfloat16),
            pltpu.VMEM((depth + scans, 2) + square, jnp.bfloat16),
            pltpu.VMEM((depth, 2) + square, jnp.bfloat16),
            pltpu.VMEM((depth + 1, 2) + square, jnp.bfloat16),
            pltpu.VMEM((5, 2) + square, jnp.bfloat16),
            pltpu.VMEM((4,) + square, jnp.float32),
            pltpu.SemaphoreType.DMA((7,)),
            pltpu.SemaphoreType.DMA((chips,)),
            pltpu.SemaphoreType.DMA((chips,)),
            pltpu.SemaphoreType.DMA((chips,)),
            pltpu.SemaphoreType.DMA((chips,)),
            pltpu.SemaphoreType.DMA((chips,)),
            pltpu.SemaphoreType.DMA((chips,)),
            pltpu.SemaphoreType.DMA((devices,)),
            pltpu.SemaphoreType.DMA((devices,)),
        ],
        compiler_params=pltpu.CompilerParams(
            collective_id=0, has_side_effects=True, vmem_limit_bytes=58 << 20
        ),
    )(
        gauge_series,
        gauge_order.reshape(devices, 1, columns),
        gauge_block.reshape(-1, LANES),
        gauge_weight.T,
        filt_trans,
        obs_gain,
        smooth_gain,
    )
    return filtered_a + filtered_b, filtered_a + smoothed_b


def solution(mesh):
    placed = (
        P("groups", "tm"),
        P(),
        P(),
        P(),
        P("groups", None),
        P("groups", None),
        P("groups", None),
    )
    return jax.shard_map(
        per_device,
        mesh=mesh,
        in_specs=placed,
        out_specs=(P(("groups", "tm"), None), P(("groups", "tm"), None)),
        check_vma=False,
    )
```
